512 devices in a mesh: row: 16 (over x, y), col: 16 (over z_lo, core), ch: 2 (over z_hi).
Axes of the slice: x: 4, y: 4, z: 16 (z_hi: 2, z_lo: 8; z = z_hi * 8 + z_lo), core: 2. Of those that a mesh axis runs over, the one named last changes fastest.
Arguments:
- image: bfloat16 [512, 512, 512], P('row', 'col', 'ch'), may hold values from -6 to 6
- weight_one: bfloat16 [3, 3, 512, 512], P(None, None, None, 'ch'), may hold values from -0.09375 to 0.09375
- scale_one: float32 [512], P('ch'), may hold values from 0.1 to 1.9
- shift_one: float32 [512], P('ch'), may hold values from -0.5 to 0.5
- weight_two: bfloat16 [3, 3, 512, 512], P(None, None, None, 'ch'), may hold values from -0.09375 to 0.09375
- scale_two: float32 [512], P('ch'), may hold values from 0.1 to 1.9
- shift_two: float32 [512], P('ch'), may hold values from -0.5 to 0.5
Outputs:
- features: bfloat16 [512, 512, 512], P('row', 'col', 'ch')
The draws below stay inside these ranges and needn't reach their ends.
All inputs are finite; a program needn't handle non-finite values.
Results may differ from the reference program's by a relative error of at most 0.0048.
Values may be sent and summed in bfloat16 or wider, within the bound.
A program may use at most 64 MiB of HBM per device.

```python
import jax
import jax.numpy as jnp
from jax import lax

CHANNELS = 512
HEIGHT = 512
WIDTH = 512


def steps_of(rng, dims, shards, low, largest):
    level, own = 1.0, jax.random.fold_in(rng, 6)
    for position, blocks in shards:
        steps = jnp.exp(jax.random.uniform(jax.random.fold_in(own, position), (blocks,), jnp.float32, low / len(shards), largest / len(shards)))
        level = level * jnp.repeat(steps, dims[position] // blocks).reshape([-1 if axis == position else 1 for axis in range(len(dims))])
    return level


def noise(rng, shape, width, most, cuts=(), kind=jnp.bfloat16):
    drawn = width * jax.random.normal(rng, shape, jnp.float32)
    if cuts:
        drawn = drawn * steps_of(rng, shape, cuts, -0.22, 0.18)
    return jnp.clip(drawn, -most, most).astype(kind)


def setup_inputs(seed: int = 0) -> dict:
    key_of = jax.random.split(jax.random.key(seed), 8)
    return {
        "image": noise(key_of[0], (HEIGHT, WIDTH, CHANNELS), 1.0, 6.0, ((0, 16), (1, 16), (2, 2))),
        "weight_one": noise(key_of[1], (3, 3, CHANNELS, CHANNELS), (9 * CHANNELS) ** -0.5, 0.09375, ((3, 2),)),
        "scale_one": jnp.clip(1.0 + 0.18 * jax.random.normal(key_of[2], (CHANNELS,), jnp.float32), 0.1, 1.9),
        "shift_one": jnp.clip(jax.random.uniform(key_of[3], (CHANNELS,), jnp.float32, -0.5, 0.5) * steps_of(key_of[3], (CHANNELS,), ((0, 2),), -0.4, 0.0), -0.5, 0.5),
        "weight_two": noise(key_of[4], (3, 3, CHANNELS, CHANNELS), (9 * CHANNELS) ** -0.5, 0.09375, ((3, 2),)),
        "scale_two": jnp.clip(1.0 + 0.18 * jax.random.normal(key_of[5], (CHANNELS,), jnp.float32), 0.1, 1.9),
        "shift_two": jnp.clip(jax.random.uniform(key_of[6], (CHANNELS,), jnp.float32, -0.5, 0.5) * steps_of(key_of[6], (CHANNELS,), ((0, 2),), -0.4, 0.0), -0.5, 0.5),
    }


def convolve(source, weight):
    result = lax.conv_general_dilated(source[None], weight, (1, 1), "SAME", dimension_numbers=("NHWC", "HWIO", "NHWC"), preferred_element_type=jnp.float32)
    return result[0]


def reference(image, weight_one, scale_one, shift_one, weight_two, scale_two, shift_two):
    conv_one = convolve(image, weight_one)
    hidden = jnp.maximum(conv_one * scale_one + shift_one, 0.0).astype(jnp.bfloat16)
    conv_two = convolve(hidden, weight_two)
    return jnp.maximum(conv_two * scale_two + shift_two, 0.0).astype(jnp.bfloat16)
```

```python
import jax
import jax.numpy as jnp
from jax import lax
from jax.experimental import pallas as pl
from jax.experimental.pallas import tpu as pltpu
from jax.sharding import PartitionSpec as P

MESH = pl.DeviceIdType.MESH
F32 = jnp.float32
BF16 = jnp.bfloat16
TILE = 32
HALF = 256
EXT = TILE + 4
HID = TILE + 2
TAPS = 9 * 2 * HALF

CHUNKS = ((0, 8), (24, 8), (8, 8), (16, 4), (20, 4))
OWN_TOP, OWN_BOTTOM, TOP, BOTTOM = 0, 1, 2, 3
GROUPS = ((0, 2), (34, 2), (0, 2), (34, 2)) + tuple((r + 2, n) for r, n in CHUNKS)
CHUNK_SLOT = 4


class Sems:
    def __init__(self, send, recv):
        self.send, self.recv, self.used = send, recv, 0

    def copy(self, src, dst, device):
        i = self.used
        self.used += 1
        return pltpu.make_async_remote_copy(
            src, dst, self.send.at[i], self.recv.at[i], device_id=device, device_id_type=MESH
        )


N_SEMS = 48


def kernel(
    rows, cols,
    img, w1_own, s1, t1, w2_own, s2, t2,
    out,
    x, hid, w1, w2, strip, edge, msg_out, msg_in, big_out, big_in, acc, result, s1all, t1all,
    send_sem, recv_sem, local_sem, out_sem,
):
    r, c, h = lax.axis_index("row"), lax.axis_index("col"), lax.axis_index("ch")
    o = 1 - h
    side = int(round(rows**0.5))
    levels = cols // 2
    px, py = r // side, r % side
    zl, core = c // 2, c % 2
    sems = Sems(send_sem, recv_sem)

    anti = (r, c, o)
    up, down = (r - 1, c, h), (r + 1, c, h)
    left, right = (r, c - 1, h), (r, c + 1, h)
    sibling = (r, zl * 2 + 1 - core, h)
    partner = (r, (levels - 1 - zl) * 2 + core, o)
    has_up, has_down, has_left, has_right = r > 0, r < rows - 1, c > 0, c < cols - 1
    border = (zl == 0) | (zl == levels - 1)
    lower = zl < levels // 2
    outer_z = jnp.where(lower, zl - 1, zl + 1)
    inner_z = jnp.where(lower, zl + 1, zl - 1)
    outer, inner = (r, outer_z * 2 + core, h), (r, inner_z * 2 + core, h)
    has_outer = jnp.logical_not(border)
    has_inner = (zl != levels // 2 - 1) & (zl != levels // 2)

    def ring_x(d):
        return (lax.rem(px + d + side, side) * side + py, c, h)

    def ring_y(d):
        return (px * side + lax.rem(py + d + side, side), c, h)

    barrier = pltpu.get_barrier_semaphore()
    always = [anti, ring_x(1), ring_x(-1), ring_y(1), ring_y(-1)]
    sometimes = [
        (has_up, up), (has_down, down), (has_left, left), (has_right, right),
        (border, partner), (has_outer, outer), (has_inner, inner),
    ]
    for device in always:
        pl.semaphore_signal(barrier, inc=1, device_id=device, device_id_type=MESH)
    count = len(always)
    for there, device in sometimes:
        count = count + jnp.where(there, 1, 0)

        @pl.when(there)
        def _():
            pl.semaphore_signal(barrier, inc=1, device_id=device, device_id_type=MESH)

    locals_ = [
        pltpu.make_async_copy(img, x.at[1, h, pl.ds(2, TILE)], local_sem.at[0]),
        pltpu.make_async_copy(w1_own, w1.at[h], local_sem.at[1]),
        pltpu.make_async_copy(w2_own, w2, local_sem.at[2]),
    ]
    for copy in locals_:
        copy.start()
    s1all[h] = s1[...]
    t1all[h] = t1[...]
    strip[...] = jnp.zeros_like(strip)
    edge[...] = jnp.zeros_like(edge)

    @pl.when(jnp.logical_not(has_up))
    def _():
        x[1, :, 0:2] = jnp.zeros((2, 2, TILE, HALF), BF16)

    @pl.when(jnp.logical_not(has_down))
    def _():
        x[1, :, EXT - 2 : EXT] = jnp.zeros((2, 2, TILE, HALF), BF16)

    pl.semaphore_wait(barrier, count)

    part = TAPS // 2 // rows
    block = part * side
    my_half, its_half = core * (TAPS // 2), (1 - core) * (TAPS // 2)

    def w_rows(start, size):
        return w1.at[o, pl.ds(pl.multiple_of(start, 16), size)]

    piece = my_half + r * part
    chain_in = sems.copy(
        w1_own.at[pl.ds(pl.multiple_of(piece, 16), part)],
        w1.at[h, pl.ds(pl.multiple_of(piece, 16), part)],
        partner,
    )

    @pl.when(border)
    def _():
        chain_in.start()

    scale_copy = sems.copy(s1, s1all.at[h], anti)
    shift_copy = sems.copy(t1, t1all.at[h], anti)
    scale_copy.start()
    shift_copy.start()
    across = [
        sems.copy(img.at[pl.ds(r0, n)], x.at[1, h, pl.ds(r0 + 2, n)], anti) for r0, n in CHUNKS
    ]
    for copy in across[:2]:
        copy.start()

    def row_copies(half, source):
        top = sems.copy(source(0), x.at[1, half, pl.ds(EXT - 2, 2)], up)
        bottom = sems.copy(source(TILE - 2), x.at[1, half, pl.ds(0, 2)], down)
        return top, bottom

    own_top, own_bottom = row_copies(h, lambda row: img.at[pl.ds(row, 2)])
    its_top, its_bottom = row_copies(o, lambda row: x.at[1, o, pl.ds(row + 2, 2)])

    @pl.when(has_up)
    def _():
        own_top.start()

    @pl.when(has_down)
    def _():
        own_bottom.start()

    column = lax.broadcasted_iota(jnp.int32, (TILE, HALF), 0)

    def extract(half, e0, n):
        @pl.loop(e0, e0 + n)
        def _(e):
            tile = x[1, half, e].astype(F32)
            here = pl.ds(e, 1)
            strip[0, 2, half, here, :] = tile[0:1]
            strip[1, 0, half, here, :] = tile[TILE - 1 : TILE]
            edge[0, 0, half, here, :] = tile[0:1]
            edge[0, 1, half, here, :] = tile[1:2]
            edge[1, 0, half, here, :] = tile[TILE - 2 : TILE - 1]
            edge[1, 1, half, here, :] = tile[TILE - 1 : TILE]

    def pack(half, e0, padded, send):
        for d in range(2):
            both = [edge[d, i, half, e0 : e0 + padded, :] for i in range(2)]
            send[d] = jnp.concatenate(both, axis=0).astype(BF16)

    def column_copies(send, land):
        return sems.copy(send.at[0], land.at[1], left), sems.copy(send.at[1], land.at[0], right)

    def start_columns(copies):
        @pl.when(has_left)
        def _():
            copies[0].start()

        @pl.when(has_right)
        def _():
            copies[1].start()

    def unpack(half, e0, n, padded, land, copies):
        @pl.when(has_left)
        def _():
            copies[1].wait_recv()
            got = land[0].astype(F32)
            strip[0, 0, half, e0 : e0 + n, :] = got[0:n]
            strip[0, 1, half, e0 : e0 + n, :] = got[padded : padded + n]

        @pl.when(has_right)
        def _():
            copies[0].wait_recv()
            got = land[1].astype(F32)
            strip[1, 1, half, e0 : e0 + n, :] = got[0:n]
            strip[1, 2, half, e0 : e0 + n, :] = got[padded : padded + n]

    def shift_columns(half, e0, n):
        @pl.loop(e0, e0 + n)
        def _(e):
            tile = x[1, half, e].astype(F32)
            before, after = strip[0, 1, half, pl.ds(e, 1), :], strip[1, 1, half, pl.ds(e, 1), :]
            x[0, half, e] = jnp.where(column == 0, before, pltpu.roll(tile, 1, 0)).astype(BF16)
            x[2, half, e] = jnp.where(column == TILE - 1, after, pltpu.roll(tile, TILE - 1, 0)).astype(BF16)

    small = [column_copies(msg_out.at[i], msg_in.at[i]) for i in range(len(GROUPS))]
    large = column_copies(big_out, big_in)

    def give(slot, half):
        e0, n = GROUPS[slot]
        extract(half, e0, n)
        pack(half, e0, 8, msg_out.at[slot])
        start_columns(small[slot])

    def take(slot, half):
        e0, n = GROUPS[slot]
        unpack(half, e0, n, 8, msg_in.at[slot], small[slot])
        shift_columns(half, e0, n)

    keep_left, keep_right = jnp.where(has_left, 1.0, 0.0), jnp.where(has_right, 1.0, 0.0)

    def conv_one(q0, n, half):
        total = None
        for a in range(3):
            for b in range(3):
                for i in range(2):
                    e0 = q0 + a
                    main = x[b, i, e0 : e0 + n].reshape(n * TILE, HALF)
                    sides = [strip[s, b, i, e0 : e0 + 8, :] for s in range(2)]
                    sides = jnp.concatenate(sides, axis=0).astype(BF16)
                    k = ((a * 3 + b) * 2 + i) * HALF
                    term = jnp.dot(
                        jnp.concatenate([main, sides], axis=0), w1[half, k : k + HALF, :], preferred_element_type=F32
                    )
                    total = term if total is None else total + term
        acc[0 : n * TILE + 16, :] = jnp.maximum(total * s1all[half] + t1all[half], 0.0)

        @pl.loop(0, n)
        def _(i):
            q = q0 + i
            outside = ((q == 0) & jnp.logical_not(has_up)) | ((q == HID - 1) & jnp.logical_not(has_down))
            keep = jnp.where(outside, 0.0, 1.0)
            tile = acc[pl.ds(pl.multiple_of(i * TILE, TILE), TILE), :] * keep
            before = acc[pl.ds(n * TILE + i, 1), :] * (keep * keep_left)
            after = acc[pl.ds(n * TILE + 8 + i, 1), :] * (keep * keep_right)
            hid[0, half, q] = jnp.where(column == 0, before, pltpu.roll(tile, 1, 0)).astype(BF16)
            hid[1, half, q] = tile.astype(BF16)
            hid[2, half, q] = jnp.where(column == TILE - 1, after, pltpu.roll(tile, TILE - 1, 0)).astype(BF16)

    out_copies = []

    def conv_two(i0, n):
        total = None
        for a in range(3):
            for b in range(3):
                for i in range(2):
                    main = hid[b, i, i0 + a : i0 + a + n].reshape(n * TILE, HALF)
                    k = ((a * 3 + b) * 2 + i) * HALF
                    term = jnp.dot(main, w2[k : k + HALF, :], preferred_element_type=F32)
                    total = term if total is None else total + term
        done = jnp.maximum(total * s2[...] + t2[...], 0.0).astype(BF16)
        result[i0 : i0 + n] = done.reshape(n, TILE, HALF)
        copy = pltpu.make_async_copy(
            result.at[pl.ds(i0, n)], out.at[pl.ds(i0, n)], out_sem.at[len(out_copies)]
        )
        copy.start()
        out_copies.append(copy)

    locals_[0].wait()
    extract(h, 2, TILE)
    pack(h, 2, TILE, big_out)
    start_columns(large)

    @pl.when(has_up)
    def _():
        own_bottom.wait_recv()

    give(OWN_TOP, h)

    @pl.when(has_down)
    def _():
        own_top.wait_recv()

    give(OWN_BOTTOM, h)

    chain_in.wait_recv()
    chain_on = pltpu.make_async_remote_copy(
        w_rows(piece, part), w_rows(piece, part), send_sem.at[sems.used], recv_sem.at[0],
        device_id=inner, device_id_type=MESH,
    )
    sems.used += 1

    @pl.when(has_inner)
    def _():
        chain_on.start()

    def y_piece(d):
        return w_rows(my_half + px * block + lax.rem(py + d + side, side) * part, part)

    def x_block(d, lo=0, hi=block):
        return w_rows(my_half + lax.rem(px + d + side, side) * block + lo, hi - lo)

    def same(ref, device):
        return sems.copy(ref, ref, device)

    y_on = same(y_piece(0), ring_y(1)), same(y_piece(0), ring_y(-1))
    for copy in y_on:
        copy.start()

    unpack(h, 2, TILE, TILE, big_in, large)
    shift_columns(h, 2, TILE)
    take(OWN_TOP, h)
    take(OWN_BOTTOM, h)

    for copy in across[2:]:
        copy.start()

    y_on[0].wait_recv()
    y_far = same(y_piece(-1), ring_y(1))
    y_far.start()
    y_on[1].wait_recv()
    y_far.wait_recv()
    x_on = same(x_block(0), ring_x(1)), same(x_block(0), ring_x(-1))
    for copy in x_on:
        copy.start()
    to_sibling = [same(x_block(d), sibling) for d in (0, -1, 1, 2)]
    to_sibling[0].start()

    across[0].wait_recv()

    @pl.when(has_up)
    def _():
        its_top.start()

    give(CHUNK_SLOT, o)

    x_on[0].wait_recv()
    x_far = same(x_block(-1, 0, block // 2), ring_x(1)), same(x_block(1, block // 2, block), ring_x(-1))
    x_far[0].start()
    to_sibling[1].start()
    x_on[1].wait_recv()
    x_far[1].start()
    to_sibling[2].start()

    across[1].wait_recv()

    @pl.when(has_down)
    def _():
        its_bottom.start()

    give(CHUNK_SLOT + 1, o)

    for copy in x_far:
        copy.wait_recv()
    to_sibling[3].start()

    @pl.when(has_up)
    def _():
        its_bottom.wait_recv()

    give(TOP, o)

    @pl.when(has_down)
    def _():
        its_top.wait_recv()

    give(BOTTOM, o)
    take(CHUNK_SLOT, o)
    take(TOP, o)
    take(CHUNK_SLOT + 1, o)
    take(BOTTOM, o)
    for copy in locals_[1:]:
        copy.wait()
    conv_one(0, 8, h)
    conv_one(26, 8, h)
    for copy in to_sibling:
        copy.wait_recv()
    scale_copy.wait_recv()
    shift_copy.wait_recv()
    conv_one(0, 8, o)
    conv_one(26, 8, o)
    conv_two(0, 6)
    conv_two(26, 6)

    for i, (q0, n, i0, m) in enumerate(((8, 8, 6, 8), (16, 4, 14, 4), (20, 6, 18, 8))):
        across[2 + i].wait_recv()
        give(CHUNK_SLOT + 2 + i, o)
        take(CHUNK_SLOT + 2 + i, o)
        conv_one(q0, n, h)
        conv_one(q0, n, o)
        conv_two(i0, m)

    for copy in (scale_copy, shift_copy, *across, *y_on, y_far, *x_on, *x_far, *to_sibling):
        copy.wait_send()
    pairs = [(border, chain_in), (has_inner, chain_on)]
    pairs += [(has_up, own_top), (has_down, own_bottom), (has_up, its_top), (has_down, its_bottom)]
    for copies in (*small, large):
        pairs += [(has_left, copies[0]), (has_right, copies[1])]
    for there, copy in pairs:

        @pl.when(there)
        def _():
            copy.wait_send()

    for copy in out_copies:
        copy.wait()


def shards(rows, cols, image, weight_one, scale_one, shift_one, weight_two, scale_two, shift_two):
    def body(*refs):
        kernel(rows, cols, *refs)

    vmem, anywhere = pl.BlockSpec(memory_space=pltpu.VMEM), pl.BlockSpec(memory_space=pl.ANY)
    flops = 2 * TILE * TILE * TAPS * HALF * 3
    return pl.pallas_call(
        body,
        name="two_convolutions",
        out_shape=jax.ShapeDtypeStruct((TILE, TILE, HALF), BF16),
        in_specs=[anywhere, anywhere, vmem, vmem, anywhere, vmem, vmem],
        out_specs=anywhere,
        scratch_shapes=[
            pltpu.VMEM((3, 2, EXT, TILE, HALF), BF16),
            pltpu.VMEM((3, 2, HID, TILE, HALF), BF16),
            pltpu.VMEM((2, TAPS, HALF), BF16),
            pltpu.VMEM((TAPS, HALF), BF16),
            pltpu.VMEM((2, 3, 2, 48, HALF), F32),
            pltpu.VMEM((2, 2, 2, 48, HALF), F32),
            pltpu.VMEM((len(GROUPS), 2, 16, HALF), BF16),
            pltpu.VMEM((len(GROUPS), 2, 16, HALF), BF16),
            pltpu.VMEM((2, 2 * TILE, HALF), BF16),
            pltpu.VMEM((2, 2 * TILE, HALF), BF16),
            pltpu.VMEM((8 * TILE + 16, HALF), F32),
            pltpu.VMEM((TILE, TILE, HALF), BF16),
            pltpu.VMEM((2, 1, HALF), F32),
            pltpu.VMEM((2, 1, HALF), F32),
            pltpu.SemaphoreType.DMA((N_SEMS,)),
            pltpu.SemaphoreType.DMA((N_SEMS,)),
            pltpu.SemaphoreType.DMA((3,)),
            pltpu.SemaphoreType.DMA((8,)),
        ],
        compiler_params=pltpu.CompilerParams(
            collective_id=0, has_side_effects=True, vmem_limit_bytes=48 * 1024 * 1024
        ),
        cost_estimate=pl.CostEstimate(flops=flops, bytes_accessed=6_000_000, transcendentals=0),
    )(
        image,
        weight_one.reshape(TAPS, HALF),
        scale_one.reshape(1, HALF),
        shift_one.reshape(1, HALF),
        weight_two.reshape(TAPS, HALF),
        scale_two.reshape(1, HALF),
        shift_two.reshape(1, HALF),
    )


def solution(mesh):
    rows, cols = mesh.shape["row"], mesh.shape["col"]

    def local(*arrays):
        return shards(rows, cols, *arrays)

    return jax.shard_map(
        local,
        mesh=mesh,
        in_specs=(
            P("row", "col", "ch"),
            P(None, None, None, "ch"),
            P("ch"),
            P("ch"),
            P(None, None, None, "ch"),
            P("ch"),
            P("ch"),
        ),
        out_specs=P("row", "col", "ch"),
        check_vma=False,
    )
```

```python
import jax
import jax.numpy as jnp
from jax import lax
from jax.experimental import pallas as pl
from jax.experimental.pallas import tpu as pltpu
from jax.sharding import PartitionSpec as P

MESH = pl.DeviceIdType.MESH
F32 = jnp.float32
BF16 = jnp.bfloat16
TILE = 32
HALF = 256
EXT = TILE + 4
HID = TILE + 2
TAPS = 9 * 2 * HALF

CHUNKS = ((0, 8), (24, 8), (8, 8), (16, 4), (20, 4))
OWN_TOP, OWN_BOTTOM, TOP, BOTTOM = 0, 1, 2, 3
GROUPS = ((0, 2), (34, 2), (0, 2), (34, 2)) + tuple((r + 2, n) for r, n in CHUNKS)
CHUNK_SLOT = 4


class Sems:
    def __init__(self, send, recv):
        self.send, self.recv, self.used = send, recv, 0

    def copy(self, src, dst, device):
        i = self.used
        self.used += 1
        return pltpu.make_async_remote_copy(
            src, dst, self.send.at[i], self.recv.at[i], device_id=device, device_id_type=MESH
        )


class Parts:
    def __init__(self, sems, source, target, start, size, parts, device):
        self.whole = sems.copy(rows_of(source, start, size), rows_of(target, start, size), device)
        self.cuts = [
            pltpu.make_async_remote_copy(
                rows_of(source, start + i * (size // parts), size // parts),
                rows_of(target, start + i * (size // parts), size // parts),
                sems.send.at[sems.used - 1],
                sems.recv.at[sems.used - 1],
                device_id=device,
                device_id_type=MESH,
            )
            for i in range(parts)
        ]

    def start(self):
        for cut in self.cuts:
            cut.start()

    def wait_recv(self):
        self.whole.wait_recv()

    def wait_send(self):
        self.whole.wait_send()


def rows_of(ref, start, size):
    return ref.at[pl.ds(pl.multiple_of(start, 16), size)]


N_SEMS = 64
UNIT = 2
AHEAD = 2
FIRST = 3


def kernel(
    rows, cols,
    img, w1_own, s1, t1, w2_own, s2, t2,
    out,
    x, hid, w1, w2, strip, edge, msg_out, msg_in, big_out, big_in, result, s1all, t1all, s2in, t2in,
    send_sem, recv_sem, unit_sem, local_sem, out_sem,
):
    r, c, h = lax.axis_index("row"), lax.axis_index("col"), lax.axis_index("ch")
    o = 1 - h
    side = int(round(rows**0.5))
    levels = cols // 2
    px, py = r // side, r % side
    zl, core = c // 2, c % 2
    sems = Sems(send_sem, recv_sem)

    anti = (r, c, o)
    up, down = (r - 1, c, h), (r + 1, c, h)
    left, right = (r, c - 1, h), (r, c + 1, h)
    sibling = (r, zl * 2 + 1 - core, h)
    partner = (r, (levels - 1 - zl) * 2 + core, o)
    has_up, has_down, has_left, has_right = r > 0, r < rows - 1, c > 0, c < cols - 1
    border = (zl == 0) | (zl == levels - 1)
    lower = zl < levels // 2
    outer_z = jnp.where(lower, zl - 1, zl + 1)
    inner_z = jnp.where(lower, zl + 1, zl - 1)
    outer, inner = (r, outer_z * 2 + core, h), (r, inner_z * 2 + core, h)
    hop = jnp.where(lower, zl, levels - 1 - zl)
    has_outer, has_inner = hop == 1, border
    straight = hop >= 2

    def ring_x(d):
        return (lax.rem(px + d + side, side) * side + py, c, h)

    def ring_y(d):
        return (px * side + lax.rem(py + d + side, side), c, h)

    barrier = pltpu.get_barrier_semaphore()
    always = [anti, *(ring_x(d) for d in (1, -1, 2)), *(ring_y(d) for d in (1, -1, 2))]
    sometimes = [
        (has_up, up), (has_down, down), (has_left, left), (has_right, right),
        (border, partner), (has_outer, outer), (has_inner, inner),
    ]
    for device in always:
        pl.semaphore_signal(barrier, inc=1, device_id=device, device_id_type=MESH)
    count = len(always)
    for there, device in sometimes:
        count = count + jnp.where(there, 1, 0)

        @pl.when(there)
        def _():
            pl.semaphore_signal(barrier, inc=1, device_id=device, device_id_type=MESH)

    locals_ = [
        pltpu.make_async_copy(img, x.at[1, h, pl.ds(2, TILE)], local_sem.at[0]),
        pltpu.make_async_copy(w1_own, w1.at[h], local_sem.at[1]),
        pltpu.make_async_copy(w2_own, w2, local_sem.at[2]),
        pltpu.make_async_copy(s1, s1all.at[h], local_sem.at[3]),
        pltpu.make_async_copy(t1, t1all.at[h], local_sem.at[4]),
        pltpu.make_async_copy(s2, s2in, local_sem.at[5]),
        pltpu.make_async_copy(t2, t2in, local_sem.at[6]),
    ]
    for copy in locals_:
        copy.start()
    strip[...] = jnp.zeros_like(strip)
    edge[...] = jnp.zeros_like(edge)

    @pl.when(jnp.logical_not(has_up))
    def _():
        x[1, :, 0:2] = jnp.zeros((2, 2, TILE, HALF), BF16)

    @pl.when(jnp.logical_not(has_down))
    def _():
        x[1, :, EXT - 2 : EXT] = jnp.zeros((2, 2, TILE, HALF), BF16)

    column = lax.broadcasted_iota(jnp.int32, (TILE, HALF), 0)

    def extract(half, e0, n):
        @pl.loop(e0, e0 + n)
        def _(e):
            tile = x[1, half, e].astype(F32)
            here = pl.ds(e, 1)
            strip[0, 2, half, here, :] = tile[0:1]
            strip[1, 0, half, here, :] = tile[TILE - 1 : TILE]
            edge[0, 0, half, here, :] = tile[0:1]
            edge[0, 1, half, here, :] = tile[1:2]
            edge[1, 0, half, here, :] = tile[TILE - 2 : TILE - 1]
            edge[1, 1, half, here, :] = tile[TILE - 1 : TILE]

    def pack(half, e0, padded, send):
        for d in range(2):
            both = [edge[d, i, half, e0 : e0 + padded, :] for i in range(2)]
            send[d] = jnp.concatenate(both, axis=0).astype(BF16)

    def column_copies(send, land):
        return sems.copy(send.at[0], land.at[1], left), sems.copy(send.at[1], land.at[0], right)

    def start_columns(copies):
        @pl.when(has_left)
        def _():
            copies[0].start()

        @pl.when(has_right)
        def _():
            copies[1].start()

    def unpack(half, e0, n, padded, land, copies):
        @pl.when(has_left)
        def _():
            copies[1].wait_recv()
            got = land[0].astype(F32)
            strip[0, 0, half, e0 : e0 + n, :] = got[0:n]
            strip[0, 1, half, e0 : e0 + n, :] = got[padded : padded + n]

        @pl.when(has_right)
        def _():
            copies[0].wait_recv()
            got = land[1].astype(F32)
            strip[1, 1, half, e0 : e0 + n, :] = got[0:n]
            strip[1, 2, half, e0 : e0 + n, :] = got[padded : padded + n]

    def shift_columns(half, e0, n):
        @pl.loop(e0, e0 + n)
        def _(e):
            tile = x[1, half, e].astype(F32)
            before, after = strip[0, 1, half, pl.ds(e, 1), :], strip[1, 1, half, pl.ds(e, 1), :]
            x[0, half, e] = jnp.where(column == 0, before, pltpu.roll(tile, 1, 0)).astype(BF16)
            x[2, half, e] = jnp.where(column == TILE - 1, after, pltpu.roll(tile, TILE - 1, 0)).astype(BF16)

    def give(slot, half):
        e0, n = GROUPS[slot]
        extract(half, e0, n)
        pack(half, e0, 8, msg_out.at[slot])
        start_columns(small[slot])

    def take(slot, half):
        e0, n = GROUPS[slot]
        unpack(half, e0, n, 8, msg_in.at[slot], small[slot])
        shift_columns(half, e0, n)

    keep_left, keep_right = jnp.where(has_left, 1.0, 0.0), jnp.where(has_right, 1.0, 0.0)

    def conv_one(q0, n, half):
        total = None
        for a in range(3):
            for b in range(3):
                for i in range(2):
                    e0 = q0 + a
                    main = x[b, i, e0 : e0 + n].reshape(n * TILE, HALF)
                    sides = [strip[s, b, i, e0 : e0 + 8, :] for s in range(2)]
                    sides = jnp.concatenate(sides, axis=0).astype(BF16)
                    k = ((a * 3 + b) * 2 + i) * HALF
                    term = jnp.dot(
                        jnp.concatenate([main, sides], axis=0), w1[half, k : k + HALF, :], preferred_element_type=F32
                    )
                    total = term if total is None else total + term
        value = jnp.maximum(total * s1all[half] + t1all[half], 0.0)
        for i in range(n):
            q = q0 + i
            tile = value[i * TILE : (i + 1) * TILE]
            before = value[n * TILE + i : n * TILE + i + 1] * keep_left
            after = value[n * TILE + 8 + i : n * TILE + 9 + i] * keep_right
            if q in (0, HID - 1):
                keep = jnp.where(has_up if q == 0 else has_down, 1.0, 0.0)
                tile, before, after = tile * keep, before * keep, after * keep
            hid[0, half, q] = jnp.where(column == 0, before, pltpu.roll(tile, 1, 0)).astype(BF16)
            hid[1, half, q] = tile.astype(BF16)
            hid[2, half, q] = jnp.where(column == TILE - 1, after, pltpu.roll(tile, TILE - 1, 0)).astype(BF16)

    out_copies = []

    def conv_two(i0, n):
        total = None
        for a in range(3):
            for b in range(3):
                for i in range(2):
                    main = hid[b, i, i0 + a : i0 + a + n].reshape(n * TILE, HALF)
                    k = ((a * 3 + b) * 2 + i) * HALF
                    term = jnp.dot(main, w2[k : k + HALF, :], preferred_element_type=F32)
                    total = term if total is None else total + term
        done = jnp.maximum(total * s2in[...] + t2in[...], 0.0).astype(BF16)
        result[i0 : i0 + n] = done.reshape(n, TILE, HALF)
        copy = pltpu.make_async_copy(
            result.at[pl.ds(i0, n)], out.at[pl.ds(i0, n)], out_sem.at[len(out_copies)]
        )
        copy.start()
        out_copies.append(copy)

    locals_[0].wait()
    extract(h, 2, TILE)
    pack(h, 2, TILE, big_out)

    pl.semaphore_wait(barrier, count)

    part = TAPS // 2 // rows
    block = part * side
    my_half = core * (TAPS // 2)
    near_pos, far_pos = jnp.where(core == 0, py, px), jnp.where(core == 0, px, py)
    piece = my_half + far_pos * block + near_pos * part

    def ring(d, first):
        along_y = (core == 0) if first else (core == 1)
        qx = jnp.where(along_y, px, lax.rem(px + d + side, side))
        qy = jnp.where(along_y, lax.rem(py + d + side, side), py)
        return (qx * side + qy, c, h)

    chain_in = Parts(sems, w1_own, w1.at[h], piece, part, 3, partner)
    chain_on = Parts(Sems(send_sem.at[pl.ds(sems.used, 1)], recv_sem.at[pl.ds(0, 1)]), w1.at[o], w1.at[o], piece, part, 3, inner)
    sems.used += 1

    chain_far = Parts(Sems(send_sem.at[pl.ds(sems.used, 1)], recv_sem.at[pl.ds(0, 1)]), w1_own, w1.at[h], piece, part, 3, anti)
    sems.used += 1

    @pl.when(border)
    def _():
        chain_in.start()

    @pl.when(straight)
    def _():
        chain_far.start()

    scale_copy = sems.copy(s1, s1all.at[h], anti)
    shift_copy = sems.copy(t1, t1all.at[h], anti)
    scale_copy.start()
    shift_copy.start()

    def row_copies(half, source):
        top = sems.copy(source(0), x.at[1, half, pl.ds(EXT - 2, 2)], up)
        bottom = sems.copy(source(TILE - 2), x.at[1, half, pl.ds(0, 2)], down)
        return top, bottom

    own_top, own_bottom = row_copies(h, lambda row: img.at[pl.ds(row, 2)])
    its_top, its_bottom = row_copies(o, lambda row: x.at[1, o, pl.ds(row + 2, 2)])

    @pl.when(has_up)
    def _():
        own_top.start()

    @pl.when(has_down)
    def _():
        own_bottom.start()

    small = [column_copies(msg_out.at[i], msg_in.at[i]) for i in range(len(GROUPS))]
    large = column_copies(big_out, big_in)
    start_columns(large)

    across, units = [], []
    for r0, n in CHUNKS:
        chunk = sems.copy(img.at[pl.ds(r0, n)], x.at[1, h, pl.ds(r0 + 2, n)], anti)
        across.append(chunk)
        for row in range(r0, r0 + n, UNIT):
            sem = sems.used - 1
            units.append(
                pltpu.make_async_remote_copy(
                    img.at[pl.ds(row, UNIT)], x.at[1, h, pl.ds(row + 2, UNIT)],
                    unit_sem.at[len(units)], recv_sem.at[sem], device_id=anti, device_id_type=MESH,
                )
            )
    sent = [0]

    def pump(n):
        for _ in range(n * 2 // UNIT):
            if sent[0] < len(units):
                if sent[0] >= AHEAD:
                    units[sent[0] - AHEAD].wait_send()
                units[sent[0]].start()
                sent[0] += 1

    pump(FIRST)

    @pl.when(has_up)
    def _():
        own_bottom.wait_recv()

    give(OWN_TOP, h)

    @pl.when(has_down)
    def _():
        own_top.wait_recv()

    give(OWN_BOTTOM, h)

    mine = my_half + far_pos * block
    first_on = [Parts(sems, w1.at[o], w1.at[o], piece, part, 3, ring(d, True)) for d in (1, -1, 2)]
    second_on = [Parts(sems, w1.at[o], w1.at[o], mine, block, 4, ring(d, False)) for d in (1, -1, 2)]
    near = Parts(sems, w1.at[o], w1.at[o], mine, block, 4, sibling)
    far = [
        Parts(sems, w1.at[o], w1.at[o], my_half + lax.rem(far_pos + d + side, side) * block, block, 4, sibling)
        for d in (-1, 1, 2)
    ]

    def weights_here():
        chain_in.wait_recv()

        @pl.when(has_inner)
        def _():
            chain_on.start()

        for copy in first_on:
            copy.start()

    @pl.when(border)
    def _():
        weights_here()

    pump(1)

    @pl.when(jnp.logical_not(border))
    def _():
        weights_here()

    pump(1)
    unpack(h, 2, TILE, TILE, big_in, large)
    shift_columns(h, 2, TILE)
    take(OWN_TOP, h)
    take(OWN_BOTTOM, h)
    pump(1)
    for copy in first_on:
        copy.wait_recv()
    for copy in second_on:
        copy.start()
    near.start()
    pump(1)

    across[0].wait_recv()

    @pl.when(has_up)
    def _():
        its_top.start()

    give(CHUNK_SLOT, o)
    pump(4)
    across[1].wait_recv()

    @pl.when(has_down)
    def _():
        its_bottom.start()

    give(CHUNK_SLOT + 1, o)
    for copy, on in zip(second_on, far):
        copy.wait_recv()
        on.start()

    @pl.when(has_up)
    def _():
        its_bottom.wait_recv()

    give(TOP, o)

    @pl.when(has_down)
    def _():
        its_top.wait_recv()

    give(BOTTOM, o)
    pump(1)
    take(CHUNK_SLOT, o)
    take(TOP, o)
    for copy in locals_[1:]:
        copy.wait()
    conv_one(0, 8, h)
    pump(1)
    take(CHUNK_SLOT + 1, o)
    take(BOTTOM, o)
    conv_one(26, 8, h)
    pump(1)
    scale_copy.wait_recv()
    shift_copy.wait_recv()
    pump(1)
    for copy in (near, *far):
        copy.wait_recv()
    conv_one(0, 8, o)
    pump(1)
    conv_two(0, 6)
    pump(1)
    conv_one(26, 8, o)
    pump(1)
    conv_two(26, 6)
    pump(len(units))
    last = CHUNK_SLOT + 2
    across[2].wait_recv()
    give(last, o)
    across[3].wait_recv()
    give(last + 1, o)
    take(last, o)
    conv_one(8, 8, h)
    across[4].wait_recv()
    give(last + 2, o)
    conv_one(8, 8, o)
    take(last + 1, o)
    conv_one(16, 4, h)
    conv_one(16, 4, o)
    conv_two(6, 12)
    take(last + 2, o)
    conv_one(20, 6, h)
    conv_one(20, 6, o)
    conv_two(18, 8)

    for copy in (scale_copy, shift_copy, *units[-AHEAD:], *first_on, *second_on, near, *far):
        copy.wait_send()
    pairs = [(border, chain_in), (straight, chain_far), (has_inner, chain_on)]
    pairs += [(has_up, own_top), (has_down, own_bottom), (has_up, its_top), (has_down, its_bottom)]
    for copies in (*small, large):
        pairs += [(has_left, copies[0]), (has_right, copies[1])]
    for there, copy in pairs:

        @pl.when(there)
        def _():
            copy.wait_send()

    for copy in out_copies:
        copy.wait()


def shards(rows, cols, image, weight_one, scale_one, shift_one, weight_two, scale_two, shift_two):
    def body(*refs):
        kernel(rows, cols, *refs)

    hbm = pl.BlockSpec(memory_space=pltpu.HBM)
    flops = 2 * TILE * TILE * TAPS * HALF * 3
    return pl.pallas_call(
        body,
        name="two_convolutions",
        out_shape=jax.ShapeDtypeStruct((TILE, TILE, HALF), BF16),
        in_specs=[hbm] * 7,
        out_specs=hbm,
        scratch_shapes=[
            pltpu.VMEM((3, 2, EXT, TILE, HALF), BF16),
            pltpu.VMEM((3, 2, HID, TILE, HALF), BF16),
            pltpu.VMEM((2, TAPS, HALF), BF16),
            pltpu.VMEM((TAPS, HALF), BF16),
            pltpu.VMEM((2, 3, 2, 48, HALF), F32),
            pltpu.VMEM((2, 2, 2, 48, HALF), F32),
            pltpu.VMEM((len(GROUPS), 2, 16, HALF), BF16),
            pltpu.VMEM((len(GROUPS), 2, 16, HALF), BF16),
            pltpu.VMEM((2, 2 * TILE, HALF), BF16),
            pltpu.VMEM((2, 2 * TILE, HALF), BF16),
            pltpu.VMEM((TILE, TILE, HALF), BF16),
            pltpu.VMEM((2, 1, HALF), F32),
            pltpu.VMEM((2, 1, HALF), F32),
            pltpu.VMEM((1, HALF), F32),
            pltpu.VMEM((1, HALF), F32),
            pltpu.SemaphoreType.DMA((N_SEMS,)),
            pltpu.SemaphoreType.DMA((N_SEMS,)),
            pltpu.SemaphoreType.DMA((TILE // UNIT,)),
            pltpu.SemaphoreType.DMA((7,)),
            pltpu.SemaphoreType.DMA((8,)),
        ],
        compiler_params=pltpu.CompilerParams(
            collective_id=0, has_side_effects=True, vmem_limit_bytes=64 * 1024 * 1024 - 65536
        ),
        cost_estimate=pl.CostEstimate(flops=flops, bytes_accessed=6_000_000, transcendentals=0),
    )(
        image,
        weight_one.reshape(TAPS, HALF),
        scale_one.reshape(1, HALF),
        shift_one.reshape(1, HALF),
        weight_two.reshape(TAPS, HALF),
        scale_two.reshape(1, HALF),
        shift_two.reshape(1, HALF),
    )


def solution(mesh):
    rows, cols = mesh.shape["row"], mesh.shape["col"]

    def local(*arrays):
        return shards(rows, cols, *arrays)

    return jax.shard_map(
        local,
        mesh=mesh,
        in_specs=(
            P("row", "col", "ch"),
            P(None, None, None, "ch"),
            P("ch"),
            P("ch"),
            P(None, None, None, "ch"),
            P("ch"),
            P("ch"),
        ),
        out_specs=P("row", "col", "ch"),
        check_vma=False,
    )
```
